32 devices in a mesh: prow: 8 (over z, x), pcol: 4 (over y, core).
Axes of the slice: x: 2, y: 2, z: 4, core: 2. Of those that a mesh axis runs over, the one named last changes fastest.
Arguments:
- slab: float32 [4096, 2048], P('prow', 'pcol'), may hold values from -6 to 6
- panel: float32 [4096, 512], P('prow', 'pcol'), may hold values from -0.25 to 0.25
- tri_inverse: float32 [512, 512], replicated, as said below
- pivots: int32 [512], replicated, may hold values from 512 to 4095, as said below
Outputs:
- updated: float32 [4096, 2048], P('prow', 'pcol')
The draws below stay inside these ranges and needn't reach their ends.
Inputs may be any that keep to these rules, and one draw needn't show every extreme that they name: The pivots are distinct row numbers of the rows below the first 512. At most 75 of them fall among the 512 rows of one device, and some device holds exactly 75. `tri_inverse`: lower triangular with zeros above the diagonal; the diagonal lies between 0.8 and 1.2.
All inputs are finite; a program needn't handle non-finite values.
Results may differ from the reference program's by a relative error of at most 0.000053.
Values sent between devices are 32-bit elements; how exact they have to be, the bound alone decides.
No kernel may reach another device: no remote copies, remote signals or barrier semaphores. Data moves between devices by JAX's collectives and lax.ppermute only.
A program may use at most 64 MiB of HBM per device.

```python
import jax
import jax.numpy as jnp
from jax import lax

NB = 512
ROWS = 4096
COLS = 2048
PIV_MOST = 75
N_PROW = 8


def draw_pivots(key, part):
    first, second, third = jax.random.split(jax.random.fold_in(key, 11), 3)
    capacity = PIV_MOST
    slots_all = (N_PROW - 1) * capacity
    spare = jax.random.permutation(first, slots_all - 1 - capacity)[:NB - capacity - 1] + capacity
    chosen = jnp.concatenate([jnp.arange(capacity, dtype=jnp.int32), spare.astype(jnp.int32), jnp.array([slots_all - 1], jnp.int32)])
    device_row = 1 + chosen // capacity
    band = chosen % capacity
    spacing = NB // capacity
    offset = jax.random.randint(second, (NB,), 0, spacing).astype(jnp.int32)
    offset = offset.at[0].set(0)
    local_row = band * spacing + offset
    local_row = local_row.at[NB - 1].set(NB - 1)
    values = (device_row * NB + local_row).astype(jnp.int32)
    order = jax.random.permutation(third, NB)
    return values[order].astype(jnp.int32)


def draw_tri_inverse(key, part):
    first, second = jax.random.split(jax.random.fold_in(key, 23))
    lower = 0.7 * jax.random.normal(first, (NB, NB), jnp.float32) / jnp.sqrt(NB * 1.0)
    diag_vals = jax.random.uniform(second, (NB,), jnp.float32, 0.8, 1.2)
    return jnp.tril(lower, -1) + jnp.diag(diag_vals)


def block_levels(stream_key, extent, cuts, least, high):
    def one(dim, parts):
        draws = jax.random.uniform(jax.random.fold_in(jax.random.fold_in(stream_key, 6), dim), (parts,), jnp.float32, least / len(cuts), high / len(cuts))
        return jnp.repeat(jnp.exp(draws), extent[dim] // parts).reshape((-1,) + (1,) * (len(extent) - dim - 1))

    gain = one(*cuts[0])
    for cut in cuts[1:]:
        gain = gain * one(*cut)
    return gain


def noise(own_key, extent, width, reach, shards=(), kind=jnp.bfloat16):
    values = width * jax.random.normal(own_key, extent, jnp.float32)
    if shards:
        values = values * block_levels(own_key, extent, shards, -0.22, 0.18)
    return jnp.clip(values, -reach, reach).astype(kind)


def setup_inputs(seed: int = 0) -> dict:
    splits = jax.random.split(jax.random.key(seed), 5)
    slab = noise(splits[0], (ROWS, COLS), 1.0, 6.0, ((0, 8), (1, 4)), jnp.float32)
    panel = noise(splits[1], (ROWS, NB), NB ** -0.5, 0.25, ((0, 8), (1, 4)), jnp.float32)
    tri_inverse = draw_tri_inverse(jax.random.fold_in(splits[4], 71), 0)
    pivots = draw_pivots(jax.random.fold_in(splits[4], 71), 0)
    return {"slab": slab, "panel": panel, "tri_inverse": tri_inverse, "pivots": pivots}


def reference(slab, panel, tri_inverse, pivots):
    leading = slab[:NB]
    rows_u = slab[pivots]
    swapped = slab.at[pivots].set(leading)
    u_block = jnp.dot(tri_inverse, rows_u, precision=lax.Precision.HIGHEST, preferred_element_type=jnp.float32)
    product = jnp.dot(panel, u_block, precision=lax.Precision.HIGHEST, preferred_element_type=jnp.float32)
    updated = swapped - product
    return updated.at[:NB].set(u_block)
```

```python
import functools

import jax
import jax.numpy as jnp
from jax import lax
from jax.experimental import pallas as pl
from jax.experimental.pallas import tpu as pltpu
from jax.sharding import PartitionSpec as P

F32 = jnp.float32
BF16 = jnp.bfloat16
VMEM_BYTES = 48 * 1024 * 1024


def _two_parts(x):
    high = x.astype(BF16)
    low = (x - high.astype(F32)).astype(BF16)
    return high, low


def _three_parts(x):
    high = x.astype(BF16)
    rest = x - high.astype(F32)
    mid = rest.astype(BF16)
    low = (rest - mid.astype(F32)).astype(BF16)
    return high, mid, low


def _dot(a, b):
    return jnp.dot(a, b, preferred_element_type=F32)


def _dot_nt(a, b):
    return lax.dot_general(a, b, (((1,), (1,)), ((), ())), preferred_element_type=F32)


def _iota(shape, dim):
    return lax.broadcasted_iota(jnp.int32, shape, dim)


def _owners_and_ranks(piv, rows_dev, devices):
    count = piv.shape[1]
    owner = piv // rows_dev
    local = piv - owner * rows_dev
    is_owner = _iota((devices, count), 0) == owner
    earlier = (_iota((count, count), 0) < _iota((count, count), 1)).astype(BF16)
    ranks = _dot(is_owner.astype(BF16), earlier)
    rank = jnp.sum(jnp.where(is_owner, ranks, 0.0), axis=0, keepdims=True)
    return owner, local, rank.astype(jnp.int32)


def _select_rows(one_hot, parts):
    high, mid, low = parts
    return (_dot(one_hot, high) + _dot(one_hot, mid)) + _dot(one_hot, low)


def _outgoing_kernel(devices, block, me_ref, piv_ref, slab_ref, *out_refs):
    me = me_ref[0]
    rows_dev = slab_ref.shape[0]
    piv = piv_ref[...]
    count = piv.shape[1]
    owner, local, rank = _owners_and_ranks(piv, rows_dev, devices)
    parts = _three_parts(slab_ref[...])

    @pl.when(me == 0)
    def _():
        for step in range(1, devices):
            slot = jnp.where(owner == step, rank, -1)
            pick = (_iota((block, count), 0) == slot).astype(BF16)
            if count < rows_dev:
                pick = jnp.pad(pick, ((0, 0), (0, rows_dev - count)))
            out_refs[step][...] = _select_rows(pick, parts)
        out_refs[0][...] = jnp.zeros_like(out_refs[0])

    @pl.when(me != 0)
    def _():
        slot = jnp.where(owner == me, rank, -1)
        pick = (_iota((block, count), 0) == slot).astype(BF16)
        at_row = (_iota((rows_dev, count), 0) == local).astype(BF16)
        mine = _select_rows(_dot_nt(pick, at_row).astype(BF16), parts)
        for step in range(devices):
            out_refs[step][...] = mine


def _factor_kernel(devices, block, pieces, me_ref, col_ref, piv_ref, slab_ref, tri_ref, *refs):
    panel_refs = refs[:pieces]
    high_ref, low_ref, kept_ref, w_ref = refs[pieces:]
    me = me_ref[0]
    rows_dev = slab_ref.shape[0]
    depth = panel_refs[0].shape[1]
    piv = piv_ref[...]
    count = piv.shape[1]
    owner, local, rank = _owners_and_ranks(piv, rows_dev, devices)

    @pl.when(me == 0)
    def _():
        w_ref[...] = tri_ref[...]

    @pl.when(me != 0)
    def _():
        for step in range(pieces):
            first = pl.multiple_of((col_ref[0] ^ step) * depth, depth)
            tri_high, tri_low = _two_parts(tri_ref[pl.ds(first, depth), :])
            high, low = _two_parts(panel_refs[step][...])
            term = (_dot(high, tri_low) + _dot(low, tri_high)) + _dot(high, tri_high)
            if step == 0:
                w_ref[...] = -term
            else:
                w_ref[...] -= term

    total = devices * block
    slot = (owner ^ me) * block + rank
    place = (_iota((total, count), 0) == slot).astype(BF16)
    is_mine = owner == me
    lead_slot = jnp.where(is_mine, me * block + rank, -1)
    lead = (_iota((total, count), 0) == lead_slot).astype(BF16)
    at_row = ((_iota((rows_dev, count), 0) == local) & is_mine).astype(F32)
    high, low = _two_parts(w_ref[...])
    high_ref[...] = (_dot_nt(high, place) + _dot_nt(at_row.astype(BF16), lead)).astype(BF16)
    low_ref[...] = _dot_nt(low, place).astype(BF16)
    taken = jnp.sum(at_row, axis=1, keepdims=True)
    stays = (taken < 0.5) & (me != 0)
    kept_ref[...] = jnp.where(stays, slab_ref[...], 0.0)


def _update_kernel(devices, block, high_ref, low_ref, kept_ref, *refs):
    block_refs = refs[:devices]
    out_ref, high_rows, low_rows = refs[devices:]
    for step in range(devices):
        high, low = _two_parts(block_refs[step][...])
        high_rows[pl.ds(step * block, block), :] = high
        low_rows[pl.ds(step * block, block), :] = low
    small = _dot(high_ref[...], low_rows[...]) + _dot(low_ref[...], high_rows[...])
    out_ref[...] = kept_ref[...] + (small + _dot(high_ref[...], high_rows[...]))


def _whole(memory=pltpu.VMEM):
    return pl.BlockSpec(memory_space=memory)


def per_device(slab, panel, tri_inverse, pivots):
    rows_dev, cols_dev = slab.shape
    depth = panel.shape[1]
    count = pivots.shape[0]
    devices = lax.axis_size("prow")
    pieces = lax.axis_size("pcol")
    capacity = rows_dev // (devices - 1) + 2
    block = -(-capacity // 16) * 16
    me = lax.axis_index("prow").astype(jnp.int32).reshape(1)
    col = lax.axis_index("pcol").astype(jnp.int32).reshape(1)
    piv = pivots.reshape(1, count)
    params = pltpu.CompilerParams(vmem_limit_bytes=VMEM_BYTES)
    smem = _whole(pltpu.SMEM)
    vmem = _whole()

    outgoing = pl.pallas_call(
        functools.partial(_outgoing_kernel, devices, block),
        out_shape=[jax.ShapeDtypeStruct((block, cols_dev), F32)] * devices,
        in_specs=[smem, vmem, vmem],
        out_specs=[vmem] * devices,
        compiler_params=params,
        name="outgoing_rows",
    )(me, piv, slab)

    def swap(x, axis, size, step):
        return lax.ppermute(x, axis, [(i, i ^ step) for i in range(size)])

    rows = [outgoing[0]] + [swap(outgoing[s], "prow", devices, s) for s in range(1, devices)]

    panels = [panel] + [swap(panel, "pcol", pieces, s) for s in range(1, pieces)]

    high, low, kept = pl.pallas_call(
        functools.partial(_factor_kernel, devices, block, pieces),
        out_shape=[
            jax.ShapeDtypeStruct((rows_dev, devices * block), BF16),
            jax.ShapeDtypeStruct((rows_dev, devices * block), BF16),
            jax.ShapeDtypeStruct((rows_dev, cols_dev), F32),
        ],
        in_specs=[smem, smem, vmem, vmem, vmem] + [vmem] * pieces,
        out_specs=[vmem] * 3,
        scratch_shapes=[pltpu.VMEM((rows_dev, count), F32)],
        compiler_params=params,
        name="left_factor",
    )(me, col, piv, slab, tri_inverse, *panels)

    return pl.pallas_call(
        functools.partial(_update_kernel, devices, block),
        out_shape=jax.ShapeDtypeStruct((rows_dev, cols_dev), F32),
        in_specs=[vmem] * (3 + devices),
        out_specs=vmem,
        scratch_shapes=[pltpu.VMEM((devices * block, cols_dev), BF16)] * 2,
        compiler_params=params,
        name="update",
    )(high, low, kept, *rows)


def solution(mesh):
    return jax.shard_map(
        per_device,
        mesh=mesh,
        in_specs=(P("prow", "pcol"), P("prow", "pcol"), P(), P()),
        out_specs=P("prow", "pcol"),
        check_vma=False,
    )
```

```python
import functools

import jax
import jax.numpy as jnp
from jax import lax
from jax.experimental import pallas as pl
from jax.experimental.pallas import tpu as pltpu
from jax.sharding import PartitionSpec as P

F32 = jnp.float32
BF16 = jnp.bfloat16
VMEM_BYTES = 24 * 1024 * 1024
LOAD_PARTS = 4
STORE_PARTS = 4
ASSEMBLE_FLOPS = 20_000_000_000


def _two_parts(x):
    high = x.astype(BF16)
    low = (x - high.astype(F32)).astype(BF16)
    return high, low


def _dot(a, b):
    return jnp.dot(a, b, preferred_element_type=F32)


def _dot_nt(a, b):
    return lax.dot_general(a, b, (((1,), (1,)), ((), ())), preferred_element_type=F32)


def _iota(shape, dim):
    return lax.broadcasted_iota(jnp.int32, shape, dim)


def _owners_and_ranks(piv, rows_dev, devices):
    count = piv.shape[1]
    owner = piv // rows_dev
    local = piv - owner * rows_dev
    is_owner = _iota((devices, count), 0) == owner
    earlier = (_iota((count, count), 0) < _iota((count, count), 1)).astype(BF16)
    ranks = _dot(is_owner.astype(BF16), earlier)
    rank = jnp.sum(jnp.where(is_owner, ranks, 0.0), axis=0, keepdims=True)
    return owner, local, rank.astype(jnp.int32)


def _select_rows(one_hot, parts):
    high, low = parts
    return _dot(one_hot, high) + _dot(one_hot, low)


def _outgoing_kernel(devices, block, me_ref, piv_hbm, slab_hbm, *refs):
    out_refs = refs[:devices]
    piv_ref, slab_ref, sems = refs[devices:]
    me = me_ref[0]
    rows_dev = slab_ref.shape[0]
    part = rows_dev // LOAD_PARTS
    piv_copy = pltpu.make_async_copy(piv_hbm, piv_ref, sems.at[0])
    piv_copy.start()
    loads = []
    for i in range(LOAD_PARTS):
        rows = pl.ds(i * part, part)
        loads.append(pltpu.make_async_copy(slab_hbm.at[rows], slab_ref.at[rows], sems.at[1 + i]))
        loads[-1].start()
    piv_copy.wait()
    piv = piv_ref[...]
    count = piv.shape[1]
    owner, local, rank = _owners_and_ranks(piv, rows_dev, devices)
    for load in loads:
        load.wait()
    parts = _two_parts(slab_ref[...])

    @pl.when(me == 0)
    def _():
        total = (devices - 1) * block
        slot = (owner - 1) * block + rank
        pick = (_iota((total, count), 0) == slot).astype(BF16)
        if count < rows_dev:
            pick = jnp.pad(pick, ((0, 0), (0, rows_dev - count)))
        rows = _select_rows(pick, parts)
        for step in range(1, devices):
            out_refs[step][...] = rows[(step - 1) * block : step * block]
        out_refs[0][...] = jnp.zeros_like(out_refs[0])

    @pl.when(me != 0)
    def _():
        slot = jnp.where(owner == me, rank, -1)
        pick = (_iota((block, count), 0) == slot).astype(BF16)
        at_row = (_iota((rows_dev, count), 0) == local).astype(BF16)
        mine = _select_rows(_dot_nt(pick, at_row).astype(BF16), parts)
        for step in range(devices):
            out_refs[step][...] = mine


def _relay_kernel(step, me_ref, came_ref, own_ref, out_ref):
    me = me_ref[0]
    instead = (me == 0) | (me == step)

    @pl.when(instead)
    def _():
        out_ref[...] = own_ref[...]

    @pl.when(jnp.logical_not(instead))
    def _():
        out_ref[...] = came_ref[...]


def _factor_kernel(devices, block, order, early, pieces, me_ref, col_ref, piv_ref, slab_ref, tri_ref, *refs):
    panel_refs = refs[:pieces]
    high_early, low_early, high_late, low_late, kept_ref, panel_rel, tri_rel, w_ref = refs[pieces:]
    me = me_ref[0]
    rows_dev = slab_ref.shape[0]
    depth = panel_refs[0].shape[1]
    piv = piv_ref[...]
    count = piv.shape[1]
    owner, local, rank = _owners_and_ranks(piv, rows_dev, devices)

    @pl.when(me == 0)
    def _():
        w_ref[...] = tri_ref[...]

    @pl.when(me != 0)
    def _():
        for step in range(pieces):
            first = pl.multiple_of((col_ref[0] ^ step) * depth, depth)
            tri_rel[pl.ds(step * depth, depth), :] = tri_ref[pl.ds(first, depth), :]
            panel_rel[:, pl.ds(step * depth, depth)] = panel_refs[step][...]
        tri_high, tri_low = _two_parts(tri_rel[...])
        high, low = _two_parts(panel_rel[...])
        w_ref[...] = -((_dot(high, tri_low) + _dot(low, tri_high)) + _dot(high, tri_high))

    total = devices * block
    relative = owner ^ me
    slot = rank
    lead_first = 0
    for place, step in enumerate(order):
        slot = jnp.where(relative == step, rank + place * block, slot)
        lead_first = jnp.where(me == step, place * block, lead_first)
    place = (_iota((total, count), 0) == slot).astype(BF16)
    is_mine = owner == me
    lead_slot = jnp.where(is_mine, lead_first + rank, -1)
    lead = (_iota((total, count), 0) == lead_slot).astype(BF16)
    at_row = ((_iota((rows_dev, count), 0) == local) & is_mine).astype(F32)
    high, low = _two_parts(w_ref[...])
    at_row_bf16 = at_row.astype(BF16)
    split = early * block
    for rows, high_ref, low_ref in ((slice(0, split), high_early, low_early), (slice(split, total), high_late, low_late)):
        high_ref[...] = (_dot_nt(high, place[rows]) + _dot_nt(at_row_bf16, lead[rows])).astype(BF16)
        low_ref[...] = _dot_nt(low, place[rows]).astype(BF16)
    taken = jnp.sum(at_row, axis=1, keepdims=True)
    stays = (taken < 0.5) & (me != 0)
    kept_ref[...] = jnp.where(stays, slab_ref[...], 0.0)


def _split_rows(block, block_refs, high_rows, low_rows):
    for step, ref in enumerate(block_refs):
        high, low = _two_parts(ref[...])
        high_rows[pl.ds(step * block, block), :] = high
        low_rows[pl.ds(step * block, block), :] = low


def _product(high, low, high_rows, low_rows):
    return (_dot(high, low_rows) + _dot(low, high_rows)) + _dot(high, high_rows)


def _assemble_kernel(block, blocks, *refs):
    high_rows, low_rows = refs[blocks:]
    _split_rows(block, refs[:blocks], high_rows, low_rows)


def _early_kernel(high_ref, low_ref, kept_ref, high_rows, low_rows, out_ref):
    out_ref[...] = kept_ref[...] + _product(high_ref[...], low_ref[...], high_rows[...], low_rows[...])


def _late_kernel(block, blocks, high_ref, low_ref, base_ref, *refs):
    out_hbm, high_rows, low_rows, result, sems = refs[blocks:]
    _split_rows(block, refs[:blocks], high_rows, low_rows)
    high, low = high_rows[...], low_rows[...]
    part = result.shape[0] // STORE_PARTS
    stores = []
    for i in range(STORE_PARTS):
        rows = pl.ds(i * part, part)
        result[rows, :] = base_ref[rows, :] + _product(high_ref[rows, :], low_ref[rows, :], high, low)
        stores.append(pltpu.make_async_copy(result.at[rows], out_hbm.at[rows], sems.at[i]))
        stores[-1].start()
    for store in stores:
        store.wait()


def per_device(slab, panel, tri_inverse, pivots):
    rows_dev, cols_dev = slab.shape
    count = pivots.shape[0]
    devices = lax.axis_size("prow")
    pieces = lax.axis_size("pcol")
    capacity = rows_dev // (devices - 1) + 2
    block = -(-capacity // 16) * 16
    me = lax.axis_index("prow").astype(jnp.int32).reshape(1)
    col = lax.axis_index("pcol").astype(jnp.int32).reshape(1)
    piv = pivots.reshape(1, count)
    params = pltpu.CompilerParams(vmem_limit_bytes=VMEM_BYTES)
    smem = pl.BlockSpec(memory_space=pltpu.SMEM)
    vmem = pl.BlockSpec(memory_space=pltpu.VMEM)
    hbm = pl.BlockSpec(memory_space=pltpu.HBM)
    rows_type = jax.ShapeDtypeStruct((block, cols_dev), F32)

    outgoing = pl.pallas_call(
        functools.partial(_outgoing_kernel, devices, block),
        out_shape=[rows_type] * devices,
        in_specs=[smem, hbm, hbm],
        out_specs=[vmem] * devices,
        scratch_shapes=[
            pltpu.VMEM((1, count), jnp.int32),
            pltpu.VMEM((rows_dev, cols_dev), F32),
            pltpu.SemaphoreType.DMA((LOAD_PARTS + 1,)),
        ],
        compiler_params=params,
        name="outgoing_rows",
    )(me, piv, slab)

    def swap(x, axis, size, step):
        return lax.ppermute(x, axis, [(i, i ^ step) for i in range(size)])

    relayed = list(range(4, devices, 2))
    direct = [1, 2] + relayed + [3]
    rows = {0: outgoing[0]}
    for step in direct:
        rows[step] = swap(outgoing[step], "prow", devices, step)
    for step in relayed:
        other = step ^ 1
        passed = pl.pallas_call(
            functools.partial(_relay_kernel, step),
            out_shape=rows_type,
            in_specs=[smem, vmem, vmem],
            out_specs=vmem,
            compiler_params=params,
            name="relay",
        )(me, rows[step], outgoing[other])
        pairs = [(i, i ^ 1) for i in range(devices) if i not in (0, step)] + [(0, other), (step, 1)]
        rows[other] = lax.ppermute(passed, "prow", pairs)
    order = [0] + direct + [step ^ 1 for step in relayed]
    early = 1 + len(direct)
    late = devices - early

    panels = {0: panel}
    for step in range(2, pieces, 2):
        panels[step] = swap(panels[0], "pcol", pieces, step)
    for step in range(0, pieces, 2):
        panels[step ^ 1] = swap(panels[step], "pcol", pieces, 1)

    high_early, low_early, high_late, low_late, kept = pl.pallas_call(
        functools.partial(_factor_kernel, devices, block, order, early, pieces),
        out_shape=[jax.ShapeDtypeStruct((rows_dev, k * block), BF16) for k in (early, early, late, late)]
        + [jax.ShapeDtypeStruct((rows_dev, cols_dev), F32)],
        in_specs=[smem, smem, vmem, vmem, vmem] + [vmem] * pieces,
        out_specs=[vmem] * 5,
        scratch_shapes=[
            pltpu.VMEM((rows_dev, count), F32),
            pltpu.VMEM((count, count), F32),
            pltpu.VMEM((rows_dev, count), F32),
        ],
        compiler_params=params,
        name="left_factor",
    )(me, col, piv, slab, tri_inverse, *[panels[s] for s in range(pieces)])

    result_type = jax.ShapeDtypeStruct((rows_dev, cols_dev), F32)
    high_rows, low_rows = pl.pallas_call(
        functools.partial(_assemble_kernel, block, early),
        out_shape=[jax.ShapeDtypeStruct((early * block, cols_dev), BF16)] * 2,
        in_specs=[vmem] * early,
        out_specs=[vmem] * 2,
        compiler_params=params,
        cost_estimate=pl.CostEstimate(flops=ASSEMBLE_FLOPS, bytes_accessed=0, transcendentals=0),
        name="assemble_rows",
    )(*[rows[s] for s in order[:early]])
    partial = pl.pallas_call(
        _early_kernel,
        out_shape=result_type,
        in_specs=[vmem] * 5,
        out_specs=vmem,
        compiler_params=params,
        name="early_rows",
    )(high_early, low_early, kept, high_rows, low_rows)
    return pl.pallas_call(
        functools.partial(_late_kernel, block, late),
        out_shape=result_type,
        in_specs=[vmem] * (3 + late),
        out_specs=hbm,
        scratch_shapes=[pltpu.VMEM((late * block, cols_dev), BF16)] * 2
        + [pltpu.VMEM((rows_dev, cols_dev), F32), pltpu.SemaphoreType.DMA((STORE_PARTS,))],
        compiler_params=params,
        name="late_rows",
    )(high_late, low_late, partial, *[rows[s] for s in order[early:]])


def solution(mesh):
    return jax.shard_map(
        per_device,
        mesh=mesh,
        in_specs=(P("prow", "pcol"), P("prow", "pcol"), P(), P()),
        out_specs=P("prow", "pcol"),
        check_vma=False,
    )
```

```python
import functools

import jax
import jax.numpy as jnp
from jax import lax
from jax.experimental import pallas as pl
from jax.experimental.pallas import tpu as pltpu
from jax.sharding import PartitionSpec as P

F32 = jnp.float32
BF16 = jnp.bfloat16
VMEM_BYTES = 24 * 1024 * 1024
STORE_PARTS = 4
LANES = 128
SUBLANES = 8
PICK_US = 2
AFTER_US = 0.1
FACTOR_US = 1
RELAY_US = 20
ASSEMBLE_US = 20


def _cost(us):
    return pl.CostEstimate(flops=int(us * 1_000_000_000), bytes_accessed=0, transcendentals=0)


def _two_parts(x):
    high = x.astype(BF16)
    low = (x - high.astype(F32)).astype(BF16)
    return high, low


def _dot(a, b):
    return jnp.dot(a, b, preferred_element_type=F32)


def _dot_nt(a, b):
    return lax.dot_general(a, b, (((1,), (1,)), ((), ())), preferred_element_type=F32)


def _iota(shape, dim):
    return lax.broadcasted_iota(jnp.int32, shape, dim)


def _owners_and_ranks(piv, rows_dev, devices):
    count = piv.shape[1]
    owner = piv // rows_dev
    local = piv - owner * rows_dev
    is_owner = _iota((devices, count), 0) == owner
    earlier = (_iota((count, count), 0) < _iota((count, count), 1)).astype(BF16)
    ranks = _dot(is_owner.astype(BF16), earlier)
    rank = jnp.sum(jnp.where(is_owner, ranks, 0.0), axis=0, keepdims=True)
    return owner, local, rank.astype(jnp.int32)


def _select_rows(one_hot, parts):
    high, low = parts
    return _dot(one_hot, high) + _dot(one_hot, low)


class _Packing:
    def __init__(self, capacity, cols):
        self.tiles = cols // LANES
        self.main = capacity // SUBLANES * SUBLANES
        self.extra = capacity - self.main
        while self.extra * self.tiles % SUBLANES:
            self.extra += 1
        self.shape = ((self.main + self.extra) * self.tiles, LANES)

    def __repr__(self):
        return "packing"

    def parts(self):
        for tile in range(self.tiles):
            yield tile, tile * self.main, self.tiles * self.main + tile * self.extra

    def store(self, ref, rows):
        for tile, main_at, extra_at in self.parts():
            cols = slice(tile * LANES, (tile + 1) * LANES)
            if self.main:
                ref[pl.ds(main_at, self.main), :] = rows[: self.main, cols]
            if self.extra:
                ref[pl.ds(extra_at, self.extra), :] = rows[self.main : self.main + self.extra, cols]

    def load(self, ref, block):
        tiles = []
        for _, main_at, extra_at in self.parts():
            pieces = []
            if self.main:
                pieces.append(ref[pl.ds(main_at, self.main), :])
            if self.extra:
                pieces.append(ref[pl.ds(extra_at, self.extra), :])
            if block > self.main + self.extra:
                pieces.append(jnp.zeros((block - self.main - self.extra, LANES), F32))
            tiles.append(jnp.concatenate(pieces, axis=0))
        return jnp.concatenate(tiles, axis=1)


def _pick_kernel(devices, block, rows_dev, me_ref, piv_ref, pick_ref):
    me = me_ref[0]
    piv = piv_ref[...]
    count = piv.shape[1]
    owner, local, rank = _owners_and_ranks(piv, rows_dev, devices)

    @pl.when(me == 0)
    def _():
        slot = (owner - 1) * block + rank
        pick = (_iota(((devices - 1) * block, count), 0) == slot).astype(BF16)
        if count < rows_dev:
            pick = jnp.pad(pick, ((0, 0), (0, rows_dev - count)))
        pick_ref[...] = pick

    @pl.when(me != 0)
    def _():
        slot = jnp.where(owner == me, rank, -1)
        pick = (_iota((block, count), 0) == slot).astype(BF16)
        at_row = (_iota((rows_dev, count), 0) == local).astype(BF16)
        pick_ref[pl.ds(0, block), :] = _dot_nt(pick, at_row).astype(BF16)


def _outgoing_kernel(devices, block, packing, me_ref, pick_ref, slab_ref, *out_refs):
    me = me_ref[0]
    parts = _two_parts(slab_ref[...])

    @pl.when(me == 0)
    def _():
        rows = _select_rows(pick_ref[...], parts)
        for step in range(1, devices):
            packing.store(out_refs[step], rows[(step - 1) * block : step * block])
        out_refs[0][...] = jnp.zeros_like(out_refs[0])

    @pl.when(me != 0)
    def _():
        rows = _select_rows(pick_ref[pl.ds(0, block), :], parts)
        out_refs[0][...] = rows
        for step in range(1, devices):
            packing.store(out_refs[step], rows)


def _relay_kernel(senders, me_ref, came_ref, *refs):
    out_ref = refs[-1]
    me = me_ref[0]
    usual = me >= 0
    for sender, ref in zip(senders, refs[:-1]):
        usual = usual & (me != sender)

        @pl.when(me == sender)
        def _():
            out_ref[...] = ref[...]

    @pl.when(usual)
    def _():
        out_ref[...] = came_ref[...]


def _after_kernel(panel_ref, _, out_ref):
    out_ref[...] = panel_ref[...]


def _factor_kernel(devices, block, order, early, crossed, pieces, me_ref, col_ref, piv_ref, slab_ref, tri_ref, *refs):
    panel_refs = refs[:pieces]
    high_early, low_early, high_late, low_late, kept_ref, panel_rel, tri_rel, w_ref = refs[pieces:]
    me = me_ref[0]
    rows_dev = slab_ref.shape[0]
    depth = panel_refs[0].shape[1]
    piv = piv_ref[...]
    count = piv.shape[1]
    owner, local, rank = _owners_and_ranks(piv, rows_dev, devices)

    @pl.when(me == 0)
    def _():
        w_ref[...] = tri_ref[...]

    @pl.when(me != 0)
    def _():
        for step in range(pieces):
            first = pl.multiple_of((col_ref[0] ^ step) * depth, depth)
            tri_rel[pl.ds(step * depth, depth), :] = tri_ref[pl.ds(first, depth), :]
            panel_rel[:, pl.ds(step * depth, depth)] = panel_refs[step][...]
        tri_high, tri_low = _two_parts(tri_rel[...])
        high, low = _two_parts(panel_rel[...])
        w_ref[...] = -((_dot(high, tri_low) + _dot(low, tri_high)) + _dot(high, tri_high))

    total = devices * block
    relative = owner ^ me
    lead_step = me
    for step in crossed:
        swapped = (me == 0) | (me == 1) | (me == step) | (me == step ^ 1)
        relative = jnp.where(swapped & ((relative ^ step) < 2), relative ^ 1, relative)
        lead_step = jnp.where(swapped & ((me ^ step) < 2), me ^ 1, lead_step)
    slot = rank
    lead_first = 0
    for place, step in enumerate(order):
        slot = jnp.where(relative == step, rank + place * block, slot)
        lead_first = jnp.where(lead_step == step, place * block, lead_first)
    place = (_iota((total, count), 0) == slot).astype(BF16)
    is_mine = owner == me
    lead_slot = jnp.where(is_mine, lead_first + rank, -1)
    lead = (_iota((total, count), 0) == lead_slot).astype(BF16)
    at_row = ((_iota((rows_dev, count), 0) == local) & is_mine).astype(F32)
    high, low = _two_parts(w_ref[...])
    at_row_bf16 = at_row.astype(BF16)
    split = early * block
    for rows, high_ref, low_ref in ((slice(0, split), high_early, low_early), (slice(split, total), high_late, low_late)):
        high_ref[...] = (_dot_nt(high, place[rows]) + _dot_nt(at_row_bf16, lead[rows])).astype(BF16)
        low_ref[...] = _dot_nt(low, place[rows]).astype(BF16)
    taken = jnp.sum(at_row, axis=1, keepdims=True)
    stays = (taken < 0.5) & (me != 0)
    kept_ref[...] = jnp.where(stays, slab_ref[...], 0.0)


def _split_rows(block, packing, block_refs, high_rows, low_rows):
    for place, ref in enumerate(block_refs):
        packed = ref.shape == packing.shape
        high, low = _two_parts(packing.load(ref, block) if packed else ref[...])
        high_rows[pl.ds(place * block, block), :] = high
        low_rows[pl.ds(place * block, block), :] = low


def _product(high, low, high_rows, low_rows):
    return (_dot(high, low_rows) + _dot(low, high_rows)) + _dot(high, high_rows)


def _assemble_kernel(block, packing, blocks, *refs):
    high_rows, low_rows = refs[blocks:]
    _split_rows(block, packing, refs[:blocks], high_rows, low_rows)


def _early_kernel(high_ref, low_ref, kept_ref, high_rows, low_rows, out_ref):
    out_ref[...] = kept_ref[...] + _product(high_ref[...], low_ref[...], high_rows[...], low_rows[...])


def _late_kernel(block, packing, blocks, high_ref, low_ref, base_ref, *refs):
    out_hbm, high_rows, low_rows, result, sems = refs[blocks:]
    _split_rows(block, packing, refs[:blocks], high_rows, low_rows)
    high, low = high_rows[...], low_rows[...]
    part = result.shape[0] // STORE_PARTS
    stores = []
    for i in range(STORE_PARTS):
        rows = pl.ds(i * part, part)
        result[rows, :] = base_ref[rows, :] + _product(high_ref[rows, :], low_ref[rows, :], high, low)
        stores.append(pltpu.make_async_copy(result.at[rows], out_hbm.at[rows], sems.at[i]))
        stores[-1].start()
    for store in stores:
        store.wait()


def per_device(slab, panel, tri_inverse, pivots):
    rows_dev, cols_dev = slab.shape
    count = pivots.shape[0]
    devices = lax.axis_size("prow")
    pieces = lax.axis_size("pcol")
    capacity = rows_dev // (devices - 1) + 2
    block = -(-capacity // 16) * 16
    me = lax.axis_index("prow").astype(jnp.int32).reshape(1)
    col = lax.axis_index("pcol").astype(jnp.int32).reshape(1)
    piv = pivots.reshape(1, count)
    params = pltpu.CompilerParams(vmem_limit_bytes=VMEM_BYTES)
    smem = pl.BlockSpec(memory_space=pltpu.SMEM)
    vmem = pl.BlockSpec(memory_space=pltpu.VMEM)
    hbm = pl.BlockSpec(memory_space=pltpu.HBM)

    relayed = list(range(4, devices, 2))
    crossed = [step for step in relayed if step % 4 == 0]
    packing = _Packing(capacity, cols_dev)
    packed_type = jax.ShapeDtypeStruct(packing.shape, F32)
    pick = pl.pallas_call(
        functools.partial(_pick_kernel, devices, block, rows_dev),
        out_shape=jax.ShapeDtypeStruct(((devices - 1) * block, rows_dev), BF16),
        in_specs=[smem, vmem],
        out_specs=vmem,
        compiler_params=params,
        cost_estimate=_cost(PICK_US),
        name="pick_rows",
    )(me, piv)
    outgoing = pl.pallas_call(
        functools.partial(_outgoing_kernel, devices, block, packing),
        out_shape=[jax.ShapeDtypeStruct((block, cols_dev), F32)] + [packed_type] * (devices - 1),
        in_specs=[smem, vmem, vmem],
        out_specs=[vmem] * devices,
        compiler_params=params,
        name="outgoing_rows",
    )(me, pick, slab)

    def swap(x, axis, size, step):
        return lax.ppermute(x, axis, [(i, i ^ step) for i in range(size)])

    direct = [1, 2] + relayed + [3]
    rows = {0: outgoing[0]}
    for step in direct:
        if step in crossed:
            ends = {0: step ^ 1, 1: step, step: 1, step ^ 1: 0}
            pairs = [(i, ends.get(i, i ^ step)) for i in range(devices)]
            rows[step] = lax.ppermute(outgoing[step ^ 1], "prow", pairs)
        else:
            rows[step] = swap(outgoing[step], "prow", devices, step)
    order = [0] + direct + [step ^ 1 for step in relayed]
    early = 1 + len(direct)
    late = devices - early
    panel = pl.pallas_call(
        _after_kernel,
        out_shape=jax.ShapeDtypeStruct(panel.shape, F32),
        in_specs=[vmem, pl.BlockSpec(memory_space=pl.ANY)],
        out_specs=vmem,
        compiler_params=params,
        cost_estimate=_cost(AFTER_US),
        name="panel_after",
    )(panel, rows[2])
    panels = {0: panel}
    for step in range(2, pieces, 2):
        panels[step] = swap(panels[0], "pcol", pieces, step)
    for step in range(0, pieces, 2):
        panels[step ^ 1] = swap(panels[step], "pcol", pieces, 1)

    high_early, low_early, high_late, low_late, kept = pl.pallas_call(
        functools.partial(_factor_kernel, devices, block, order, early, crossed, pieces),
        out_shape=[jax.ShapeDtypeStruct((rows_dev, k * block), BF16) for k in (early, early, late, late)]
        + [jax.ShapeDtypeStruct((rows_dev, cols_dev), F32)],
        in_specs=[smem, smem, vmem, vmem, vmem] + [vmem] * pieces,
        out_specs=[vmem] * 5,
        scratch_shapes=[
            pltpu.VMEM((rows_dev, count), F32),
            pltpu.VMEM((count, count), F32),
            pltpu.VMEM((rows_dev, count), F32),
        ],
        compiler_params=params,
        cost_estimate=_cost(FACTOR_US),
        name="left_factor",
    )(me, col, piv, slab, tri_inverse, *[panels[s] for s in range(pieces)])

    for step in relayed:
        other = step ^ 1
        if step in crossed:
            ends = {0: step, other: 1}
            blocks = {0: outgoing[step], other: outgoing[step]}
        else:
            ends = {0: other, step: 1}
            blocks = {0: outgoing[other], step: outgoing[other]}
        passed = pl.pallas_call(
            functools.partial(_relay_kernel, list(blocks)),
            out_shape=packed_type,
            in_specs=[smem, vmem] + [vmem] * len(blocks),
            out_specs=vmem,
            compiler_params=params,
            cost_estimate=_cost(RELAY_US),
            name="relay",
        )(me, rows[step], *blocks.values())
        pairs = [(i, ends.get(i, i ^ 1)) for i in range(devices)]
        rows[other] = lax.ppermute(passed, "prow", pairs)

    result_type = jax.ShapeDtypeStruct((rows_dev, cols_dev), F32)
    high_rows, low_rows = pl.pallas_call(
        functools.partial(_assemble_kernel, block, packing, early),
        out_shape=[jax.ShapeDtypeStruct((early * block, cols_dev), BF16)] * 2,
        in_specs=[vmem] * early,
        out_specs=[vmem] * 2,
        compiler_params=params,
        cost_estimate=_cost(ASSEMBLE_US),
        name="assemble_rows",
    )(*[rows[s] for s in order[:early]])
    partial = pl.pallas_call(
        _early_kernel,
        out_shape=result_type,
        in_specs=[vmem] * 5,
        out_specs=vmem,
        compiler_params=params,
        name="early_rows",
    )(high_early, low_early, kept, high_rows, low_rows)
    return pl.pallas_call(
        functools.partial(_late_kernel, block, packing, late),
        out_shape=result_type,
        in_specs=[vmem] * (3 + late),
        out_specs=hbm,
        scratch_shapes=[pltpu.VMEM((late * block, cols_dev), BF16)] * 2
        + [pltpu.VMEM((rows_dev, cols_dev), F32), pltpu.SemaphoreType.DMA((STORE_PARTS,))],
        compiler_params=params,
        name="late_rows",
    )(high_late, low_late, partial, *[rows[s] for s in order[early:]])


def solution(mesh):
    return jax.shard_map(
        per_device,
        mesh=mesh,
        in_specs=(P("prow", "pcol"), P("prow", "pcol"), P(), P()),
        out_specs=P("prow", "pcol"),
        check_vma=False,
    )
```

```python
import functools

import jax
import jax.numpy as jnp
from jax import lax
from jax.experimental import pallas as pl
from jax.experimental.pallas import tpu as pltpu
from jax.sharding import PartitionSpec as P

F32 = jnp.float32
BF16 = jnp.bfloat16
VMEM_BYTES = 24 * 1024 * 1024
STORE_PARTS = 4
LANES = 128
SUBLANES = 8
PICK_US = 2
AFTER_US = 0.1
FACTOR_US = 1
RELAY_US = 20
ASSEMBLE_US = 20


def _cost(us):
    return pl.CostEstimate(flops=int(us * 1_000_000_000), bytes_accessed=0, transcendentals=0)


def _two_parts(x):
    high = x.astype(BF16)
    low = (x - high.astype(F32)).astype(BF16)
    return high, low


def _dot(a, b):
    return jnp.dot(a, b, preferred_element_type=F32)


def _dot_nt(a, b):
    return lax.dot_general(a, b, (((1,), (1,)), ((), ())), preferred_element_type=F32)


def _iota(shape, dim):
    return lax.broadcasted_iota(jnp.int32, shape, dim)


def _owners_and_ranks(piv, rows_dev, devices):
    count = piv.shape[1]
    owner = piv // rows_dev
    local = piv - owner * rows_dev
    is_owner = _iota((devices, count), 0) == owner
    earlier = (_iota((count, count), 0) < _iota((count, count), 1)).astype(BF16)
    ranks = _dot(is_owner.astype(BF16), earlier)
    rank = jnp.sum(jnp.where(is_owner, ranks, 0.0), axis=0, keepdims=True)
    return owner, local, rank.astype(jnp.int32)


def _select_rows(one_hot, parts):
    high, low = parts
    return _dot(one_hot, high) + _dot(one_hot, low)


class _Packing:
    def __init__(self, capacity, cols):
        self.tiles = cols // LANES
        self.main = capacity // SUBLANES * SUBLANES
        self.extra = capacity - self.main
        while self.extra * self.tiles % SUBLANES:
            self.extra += 1
        self.shape = ((self.main + self.extra) * self.tiles, LANES)

    def __repr__(self):
        return "packing"

    def parts(self):
        for tile in range(self.tiles):
            yield tile, tile * self.main, self.tiles * self.main + tile * self.extra

    def store(self, ref, rows):
        for tile, main_at, extra_at in self.parts():
            cols = slice(tile * LANES, (tile + 1) * LANES)
            if self.main:
                ref[pl.ds(main_at, self.main), :] = rows[: self.main, cols]
            if self.extra:
                ref[pl.ds(extra_at, self.extra), :] = rows[self.main : self.main + self.extra, cols]

    def load(self, ref, block):
        tiles = []
        for _, main_at, extra_at in self.parts():
            pieces = []
            if self.main:
                pieces.append(ref[pl.ds(main_at, self.main), :])
            if self.extra:
                pieces.append(ref[pl.ds(extra_at, self.extra), :])
            if block > self.main + self.extra:
                pieces.append(jnp.zeros((block - self.main - self.extra, LANES), F32))
            tiles.append(jnp.concatenate(pieces, axis=0))
        return jnp.concatenate(tiles, axis=1)


def _pick_kernel(devices, block, rows_dev, me_ref, piv_ref, pick_ref):
    me = me_ref[0]
    piv = piv_ref[...]
    count = piv.shape[1]
    owner, local, rank = _owners_and_ranks(piv, rows_dev, devices)

    @pl.when(me == 0)
    def _():
        slot = (owner - 1) * block + rank
        pick = (_iota(((devices - 1) * block, count), 0) == slot).astype(BF16)
        if count < rows_dev:
            pick = jnp.pad(pick, ((0, 0), (0, rows_dev - count)))
        pick_ref[...] = pick

    @pl.when(me != 0)
    def _():
        slot = jnp.where(owner == me, rank, -1)
        pick = (_iota((block, count), 0) == slot).astype(BF16)
        at_row = (_iota((rows_dev, count), 0) == local).astype(BF16)
        pick_ref[pl.ds(0, block), :] = _dot_nt(pick, at_row).astype(BF16)


def _outgoing_kernel(devices, block, packing, me_ref, pick_ref, slab_ref, *out_refs):
    me = me_ref[0]
    parts = _two_parts(slab_ref[...])

    @pl.when(me == 0)
    def _():
        rows = _select_rows(pick_ref[...], parts)
        for step in range(1, devices):
            packing.store(out_refs[step], rows[(step - 1) * block : step * block])
        out_refs[0][...] = jnp.zeros_like(out_refs[0])

    @pl.when(me != 0)
    def _():
        rows = _select_rows(pick_ref[pl.ds(0, block), :], parts)
        out_refs[0][...] = rows
        for step in range(1, devices):
            packing.store(out_refs[step], rows)


def _relay_kernel(senders, waits, me_ref, came_ref, *refs):
    refs = refs[waits:]
    out_ref = refs[-1]
    me = me_ref[0]
    usual = me >= 0
    for sender, ref in zip(senders, refs[:-1]):
        usual = usual & (me != sender)

        @pl.when(me == sender)
        def _():
            out_ref[...] = ref[...]

    @pl.when(usual)
    def _():
        out_ref[...] = came_ref[...]


def _after_kernel(panel_ref, _, out_ref):
    out_ref[...] = panel_ref[...]


def _factor_kernel(devices, block, order, early, crossed, pieces, me_ref, col_ref, piv_ref, slab_ref, tri_ref, *refs):
    panel_refs = refs[:pieces]
    high_early, low_early, high_late, low_late, kept_ref, panel_rel, tri_rel, w_ref = refs[pieces:]
    me = me_ref[0]
    rows_dev = slab_ref.shape[0]
    depth = panel_refs[0].shape[1]
    piv = piv_ref[...]
    count = piv.shape[1]
    owner, local, rank = _owners_and_ranks(piv, rows_dev, devices)

    @pl.when(me == 0)
    def _():
        w_ref[...] = tri_ref[...]

    @pl.when(me != 0)
    def _():
        for step in range(pieces):
            first = pl.multiple_of((col_ref[0] ^ step) * depth, depth)
            tri_rel[pl.ds(step * depth, depth), :] = tri_ref[pl.ds(first, depth), :]
            panel_rel[:, pl.ds(step * depth, depth)] = panel_refs[step][...]
        tri_high, tri_low = _two_parts(tri_rel[...])
        high, low = _two_parts(panel_rel[...])
        w_ref[...] = -((_dot(high, tri_low) + _dot(low, tri_high)) + _dot(high, tri_high))

    total = devices * block
    relative = owner ^ me
    lead_step = me
    for step in crossed:
        swapped = (me == 0) | (me == 1) | (me == step) | (me == step ^ 1)
        relative = jnp.where(swapped & ((relative ^ step) < 2), relative ^ 1, relative)
        lead_step = jnp.where(swapped & ((me ^ step) < 2), me ^ 1, lead_step)
    slot = rank
    lead_first = 0
    for place, step in enumerate(order):
        slot = jnp.where(relative == step, rank + place * block, slot)
        lead_first = jnp.where(lead_step == step, place * block, lead_first)
    place = (_iota((total, count), 0) == slot).astype(BF16)
    is_mine = owner == me
    lead_slot = jnp.where(is_mine, lead_first + rank, -1)
    lead = (_iota((total, count), 0) == lead_slot).astype(BF16)
    at_row = ((_iota((rows_dev, count), 0) == local) & is_mine).astype(F32)
    high, low = _two_parts(w_ref[...])
    at_row_bf16 = at_row.astype(BF16)
    split = early * block
    for rows, high_ref, low_ref in ((slice(0, split), high_early, low_early), (slice(split, total), high_late, low_late)):
        high_ref[...] = (_dot_nt(high, place[rows]) + _dot_nt(at_row_bf16, lead[rows])).astype(BF16)
        low_ref[...] = _dot_nt(low, place[rows]).astype(BF16)
    taken = jnp.sum(at_row, axis=1, keepdims=True)
    stays = (taken < 0.5) & (me != 0)
    kept_ref[...] = jnp.where(stays, slab_ref[...], 0.0)


def _split_rows(block, packing, block_refs, high_rows, low_rows):
    for place, ref in enumerate(block_refs):
        packed = ref.shape == packing.shape
        high, low = _two_parts(packing.load(ref, block) if packed else ref[...])
        high_rows[pl.ds(place * block, block), :] = high
        low_rows[pl.ds(place * block, block), :] = low


def _product(high, low, high_rows, low_rows):
    return (_dot(high, low_rows) + _dot(low, high_rows)) + _dot(high, high_rows)


def _assemble_kernel(block, packing, blocks, *refs):
    high_rows, low_rows = refs[blocks:]
    _split_rows(block, packing, refs[:blocks], high_rows, low_rows)


def _early_kernel(high_ref, low_ref, kept_ref, high_rows, low_rows, out_ref):
    out_ref[...] = kept_ref[...] + _product(high_ref[...], low_ref[...], high_rows[...], low_rows[...])


def _late_kernel(block, packing, blocks, high_ref, low_ref, base_ref, *refs):
    out_hbm, high_rows, low_rows, result, sems = refs[blocks:]
    _split_rows(block, packing, refs[:blocks], high_rows, low_rows)
    high, low = high_rows[...], low_rows[...]
    part = result.shape[0] // STORE_PARTS
    stores = []
    for i in range(STORE_PARTS):
        rows = pl.ds(i * part, part)
        result[rows, :] = base_ref[rows, :] + _product(high_ref[rows, :], low_ref[rows, :], high, low)
        stores.append(pltpu.make_async_copy(result.at[rows], out_hbm.at[rows], sems.at[i]))
        stores[-1].start()
    for store in stores:
        store.wait()


def per_device(slab, panel, tri_inverse, pivots):
    rows_dev, cols_dev = slab.shape
    count = pivots.shape[0]
    devices = lax.axis_size("prow")
    pieces = lax.axis_size("pcol")
    capacity = rows_dev // (devices - 1) + 2
    block = -(-capacity // 16) * 16
    me = lax.axis_index("prow").astype(jnp.int32).reshape(1)
    col = lax.axis_index("pcol").astype(jnp.int32).reshape(1)
    piv = pivots.reshape(1, count)
    params = pltpu.CompilerParams(vmem_limit_bytes=VMEM_BYTES)
    smem = pl.BlockSpec(memory_space=pltpu.SMEM)
    vmem = pl.BlockSpec(memory_space=pltpu.VMEM)
    hbm = pl.BlockSpec(memory_space=pltpu.HBM)

    relayed = list(range(4, devices, 2))
    crossed = [step for step in relayed if step % 4 == 2]
    packing = _Packing(capacity, cols_dev)
    packed_type = jax.ShapeDtypeStruct(packing.shape, F32)
    pick = pl.pallas_call(
        functools.partial(_pick_kernel, devices, block, rows_dev),
        out_shape=jax.ShapeDtypeStruct(((devices - 1) * block, rows_dev), BF16),
        in_specs=[smem, vmem],
        out_specs=vmem,
        compiler_params=params,
        cost_estimate=_cost(PICK_US),
        name="pick_rows",
    )(me, piv)
    outgoing = pl.pallas_call(
        functools.partial(_outgoing_kernel, devices, block, packing),
        out_shape=[jax.ShapeDtypeStruct((block, cols_dev), F32)] + [packed_type] * (devices - 1),
        in_specs=[smem, vmem, vmem],
        out_specs=[vmem] * devices,
        compiler_params=params,
        name="outgoing_rows",
    )(me, pick, slab)

    def swap(x, axis, size, step):
        return lax.ppermute(x, axis, [(i, i ^ step) for i in range(size)])

    direct = [1, 2] + relayed + [3]
    rows = {0: outgoing[0]}
    for step in direct:
        if step in crossed:
            ends = {0: step ^ 1, 1: step, step: 1, step ^ 1: 0}
            pairs = [(i, ends.get(i, i ^ step)) for i in range(devices)]
            rows[step] = lax.ppermute(outgoing[step ^ 1], "prow", pairs)
        else:
            rows[step] = swap(outgoing[step], "prow", devices, step)
    order = [0] + direct + [step ^ 1 for step in relayed]
    early = 1 + len(direct)
    late = devices - early
    panel = pl.pallas_call(
        _after_kernel,
        out_shape=jax.ShapeDtypeStruct(panel.shape, F32),
        in_specs=[vmem, pl.BlockSpec(memory_space=pl.ANY)],
        out_specs=vmem,
        compiler_params=params,
        cost_estimate=_cost(AFTER_US),
        name="panel_after",
    )(panel, rows[2])
    panels = {0: panel}
    for step in range(2, pieces, 2):
        panels[step] = swap(panels[0], "pcol", pieces, step)
    for step in range(0, pieces, 2):
        panels[step ^ 1] = swap(panels[step], "pcol", pieces, 1)

    high_early, low_early, high_late, low_late, kept = pl.pallas_call(
        functools.partial(_factor_kernel, devices, block, order, early, crossed, pieces),
        out_shape=[jax.ShapeDtypeStruct((rows_dev, k * block), BF16) for k in (early, early, late, late)]
        + [jax.ShapeDtypeStruct((rows_dev, cols_dev), F32)],
        in_specs=[smem, smem, vmem, vmem, vmem] + [vmem] * pieces,
        out_specs=[vmem] * 5,
        scratch_shapes=[
            pltpu.VMEM((rows_dev, count), F32),
            pltpu.VMEM((count, count), F32),
            pltpu.VMEM((rows_dev, count), F32),
        ],
        compiler_params=params,
        cost_estimate=_cost(FACTOR_US),
        name="left_factor",
    )(me, col, piv, slab, tri_inverse, *[panels[s] for s in range(pieces)])

    for step in relayed:
        other = step ^ 1
        if step in crossed:
            ends = {0: step, other: 1}
            blocks = {0: outgoing[step], other: outgoing[step]}
        else:
            ends = {0: other, step: 1}
            blocks = {0: outgoing[other], step: outgoing[other]}
        waits = [rows[1], rows[3]] if step == relayed[0] else []
        passed = pl.pallas_call(
            functools.partial(_relay_kernel, list(blocks), len(waits)),
            out_shape=packed_type,
            in_specs=[smem, vmem] + [pl.BlockSpec(memory_space=pl.ANY)] * len(waits) + [vmem] * len(blocks),
            out_specs=vmem,
            compiler_params=params,
            cost_estimate=_cost(RELAY_US),
            name="relay",
        )(me, rows[step], *waits, *blocks.values())
        pairs = [(i, ends.get(i, i ^ 1)) for i in range(devices)]
        rows[other] = lax.ppermute(passed, "prow", pairs)

    result_type = jax.ShapeDtypeStruct((rows_dev, cols_dev), F32)
    high_rows, low_rows = pl.pallas_call(
        functools.partial(_assemble_kernel, block, packing, early),
        out_shape=[jax.ShapeDtypeStruct((early * block, cols_dev), BF16)] * 2,
        in_specs=[vmem] * early,
        out_specs=[vmem] * 2,
        compiler_params=params,
        cost_estimate=_cost(ASSEMBLE_US),
        name="assemble_rows",
    )(*[rows[s] for s in order[:early]])
    partial = pl.pallas_call(
        _early_kernel,
        out_shape=result_type,
        in_specs=[vmem] * 5,
        out_specs=vmem,
        compiler_params=params,
        name="early_rows",
    )(high_early, low_early, kept, high_rows, low_rows)
    return pl.pallas_call(
        functools.partial(_late_kernel, block, packing, late),
        out_shape=result_type,
        in_specs=[vmem] * (3 + late),
        out_specs=hbm,
        scratch_shapes=[pltpu.VMEM((late * block, cols_dev), BF16)] * 2
        + [pltpu.VMEM((rows_dev, cols_dev), F32), pltpu.SemaphoreType.DMA((STORE_PARTS,))],
        compiler_params=params,
        name="late_rows",
    )(high_late, low_late, partial, *[rows[s] for s in order[early:]])


def solution(mesh):
    return jax.shard_map(
        per_device,
        mesh=mesh,
        in_specs=(P("prow", "pcol"), P("prow", "pcol"), P(), P()),
        out_specs=P("prow", "pcol"),
        check_vma=False,
    )
```

```python
import functools

import jax
import jax.numpy as jnp
from jax import lax
from jax.experimental import pallas as pl
from jax.experimental.pallas import tpu as pltpu
from jax.sharding import PartitionSpec as P

F32 = jnp.float32
BF16 = jnp.bfloat16
VMEM_BYTES = 24 * 1024 * 1024
STORE_PARTS = 4
LANES = 128
SUBLANES = 8
PICK_US = 2
AFTER_US = 0.1
FACTOR_US = 1
RELAY_US = 20
ASSEMBLE_US = 20


def _cost(us):
    return pl.CostEstimate(flops=int(us * 1_000_000_000), bytes_accessed=0, transcendentals=0)


def _two_parts(x):
    high = x.astype(BF16)
    low = (x - high.astype(F32)).astype(BF16)
    return high, low


def _dot(a, b):
    return jnp.dot(a, b, preferred_element_type=F32)


def _dot_nt(a, b):
    return lax.dot_general(a, b, (((1,), (1,)), ((), ())), preferred_element_type=F32)


def _iota(shape, dim):
    return lax.broadcasted_iota(jnp.int32, shape, dim)


def _owners_and_ranks(piv, rows_dev, devices):
    count = piv.shape[1]
    owner = piv // rows_dev
    local = piv - owner * rows_dev
    is_owner = _iota((devices, count), 0) == owner
    earlier = (_iota((count, count), 0) < _iota((count, count), 1)).astype(BF16)
    ranks = _dot(is_owner.astype(BF16), earlier)
    rank = jnp.sum(jnp.where(is_owner, ranks, 0.0), axis=0, keepdims=True)
    return owner, local, rank.astype(jnp.int32)


def _select_rows(one_hot, parts):
    high, low = parts
    return _dot(one_hot, high) + _dot(one_hot, low)


class _Packing:
    def __init__(self, capacity, cols):
        self.tiles = cols // LANES
        self.main = capacity // SUBLANES * SUBLANES
        self.extra = capacity - self.main
        while self.extra * self.tiles % SUBLANES:
            self.extra += 1
        self.shape = ((self.main + self.extra) * self.tiles, LANES)

    def __repr__(self):
        return "packing"

    def parts(self):
        for tile in range(self.tiles):
            yield tile, tile * self.main, self.tiles * self.main + tile * self.extra

    def store(self, ref, rows):
        for tile, main_at, extra_at in self.parts():
            cols = slice(tile * LANES, (tile + 1) * LANES)
            if self.main:
                ref[pl.ds(main_at, self.main), :] = rows[: self.main, cols]
            if self.extra:
                ref[pl.ds(extra_at, self.extra), :] = rows[self.main : self.main + self.extra, cols]

    def load(self, ref, block):
        tiles = []
        for _, main_at, extra_at in self.parts():
            pieces = []
            if self.main:
                pieces.append(ref[pl.ds(main_at, self.main), :])
            if self.extra:
                pieces.append(ref[pl.ds(extra_at, self.extra), :])
            if block > self.main + self.extra:
                pieces.append(jnp.zeros((block - self.main - self.extra, LANES), F32))
            tiles.append(jnp.concatenate(pieces, axis=0))
        return jnp.concatenate(tiles, axis=1)


def _pick_kernel(devices, block, rows_dev, me_ref, piv_ref, pick_ref):
    me = me_ref[0]
    piv = piv_ref[...]
    count = piv.shape[1]
    owner, local, rank = _owners_and_ranks(piv, rows_dev, devices)

    @pl.when(me == 0)
    def _():
        slot = (owner - 1) * block + rank
        pick = (_iota(((devices - 1) * block, count), 0) == slot).astype(BF16)
        if count < rows_dev:
            pick = jnp.pad(pick, ((0, 0), (0, rows_dev - count)))
        pick_ref[...] = pick

    @pl.when(me != 0)
    def _():
        slot = jnp.where(owner == me, rank, -1)
        pick = (_iota((block, count), 0) == slot).astype(BF16)
        at_row = (_iota((rows_dev, count), 0) == local).astype(BF16)
        pick_ref[pl.ds(0, block), :] = _dot_nt(pick, at_row).astype(BF16)


def _outgoing_kernel(devices, block, packing, me_ref, pick_ref, slab_ref, *out_refs):
    me = me_ref[0]
    parts = _two_parts(slab_ref[...])

    @pl.when(me == 0)
    def _():
        rows = _select_rows(pick_ref[...], parts)
        for step in range(1, devices):
            packing.store(out_refs[step], rows[(step - 1) * block : step * block])
        out_refs[0][...] = jnp.zeros_like(out_refs[0])

    @pl.when(me != 0)
    def _():
        rows = _select_rows(pick_ref[pl.ds(0, block), :], parts)
        out_refs[0][...] = rows
        for step in range(1, devices):
            packing.store(out_refs[step], rows)


def _relay_kernel(senders, waits, me_ref, came_ref, *refs):
    refs = refs[waits:]
    out_ref = refs[-1]
    me = me_ref[0]
    usual = me >= 0
    for sender, ref in zip(senders, refs[:-1]):
        usual = usual & (me != sender)

        @pl.when(me == sender)
        def _():
            out_ref[...] = ref[...]

    @pl.when(usual)
    def _():
        out_ref[...] = came_ref[...]


def _after_kernel(panel_ref, _, out_ref):
    out_ref[...] = panel_ref[...]


def _factor_kernel(devices, block, order, early, crossed, pieces, me_ref, col_ref, piv_ref, slab_ref, tri_ref, *refs):
    panel_refs = refs[:pieces]
    high_early, low_early, high_late, low_late, kept_ref, panel_rel, tri_rel, w_ref = refs[pieces:]
    me = me_ref[0]
    rows_dev = slab_ref.shape[0]
    depth = panel_refs[0].shape[1]
    piv = piv_ref[...]
    count = piv.shape[1]
    owner, local, rank = _owners_and_ranks(piv, rows_dev, devices)

    @pl.when(me == 0)
    def _():
        w_ref[...] = tri_ref[...]

    @pl.when(me != 0)
    def _():
        for step in range(pieces):
            first = pl.multiple_of((col_ref[0] ^ step) * depth, depth)
            tri_rel[pl.ds(step * depth, depth), :] = tri_ref[pl.ds(first, depth), :]
            panel_rel[:, pl.ds(step * depth, depth)] = panel_refs[step][...]
        tri_high, tri_low = _two_parts(tri_rel[...])
        high, low = _two_parts(panel_rel[...])
        w_ref[...] = -((_dot(high, tri_low) + _dot(low, tri_high)) + _dot(high, tri_high))

    total = devices * block
    relative = owner ^ me
    lead_step = me
    for step in crossed:
        swapped = (me == 0) | (me == 1) | (me == step) | (me == step ^ 1)
        relative = jnp.where(swapped & ((relative ^ step) < 2), relative ^ 1, relative)
        lead_step = jnp.where(swapped & ((me ^ step) < 2), me ^ 1, lead_step)
    slot = rank
    lead_first = 0
    for place, step in enumerate(order):
        slot = jnp.where(relative == step, rank + place * block, slot)
        lead_first = jnp.where(lead_step == step, place * block, lead_first)
    place = (_iota((total, count), 0) == slot).astype(BF16)
    is_mine = owner == me
    lead_slot = jnp.where(is_mine, lead_first + rank, -1)
    lead = (_iota((total, count), 0) == lead_slot).astype(BF16)
    at_row = ((_iota((rows_dev, count), 0) == local) & is_mine).astype(F32)
    high, low = _two_parts(w_ref[...])
    at_row_bf16 = at_row.astype(BF16)
    split = early * block
    for rows, high_ref, low_ref in ((slice(0, split), high_early, low_early), (slice(split, total), high_late, low_late)):
        high_ref[...] = (_dot_nt(high, place[rows]) + _dot_nt(at_row_bf16, lead[rows])).astype(BF16)
        low_ref[...] = _dot_nt(low, place[rows]).astype(BF16)
    taken = jnp.sum(at_row, axis=1, keepdims=True)
    stays = (taken < 0.5) & (me != 0)
    kept_ref[...] = jnp.where(stays, slab_ref[...], 0.0)


def _split_rows(block, packing, block_refs, high_rows, low_rows):
    for place, ref in enumerate(block_refs):
        packed = ref.shape == packing.shape
        high, low = _two_parts(packing.load(ref, block) if packed else ref[...])
        high_rows[pl.ds(place * block, block), :] = high
        low_rows[pl.ds(place * block, block), :] = low


def _product(high, low, high_rows, low_rows):
    return (_dot(high, low_rows) + _dot(low, high_rows)) + _dot(high, high_rows)


def _assemble_kernel(block, packing, blocks, *refs):
    high_rows, low_rows = refs[blocks:]
    _split_rows(block, packing, refs[:blocks], high_rows, low_rows)


def _early_kernel(high_ref, low_ref, kept_ref, high_rows, low_rows, out_ref):
    out_ref[...] = kept_ref[...] + _product(high_ref[...], low_ref[...], high_rows[...], low_rows[...])


def _late_kernel(block, packing, late, high_ref, low_ref, base_ref, last_ref, rest_high, rest_low, *refs):
    out_hbm, high_rows, low_rows, result, sems = refs
    rest = pl.ds(block, (late - 1) * block)
    high_rows[rest, :] = rest_high[...]
    low_rows[rest, :] = rest_low[...]
    _split_rows(block, packing, [last_ref], high_rows, low_rows)
    high, low = high_rows[...], low_rows[...]
    part = result.shape[0] // STORE_PARTS
    stores = []
    for i in range(STORE_PARTS):
        rows = pl.ds(i * part, part)
        result[rows, :] = base_ref[rows, :] + _product(high_ref[rows, :], low_ref[rows, :], high, low)
        stores.append(pltpu.make_async_copy(result.at[rows], out_hbm.at[rows], sems.at[i]))
        stores[-1].start()
    for store in stores:
        store.wait()


def per_device(slab, panel, tri_inverse, pivots):
    rows_dev, cols_dev = slab.shape
    count = pivots.shape[0]
    devices = lax.axis_size("prow")
    pieces = lax.axis_size("pcol")
    capacity = rows_dev // (devices - 1) + 2
    block = -(-capacity // 16) * 16
    me = lax.axis_index("prow").astype(jnp.int32).reshape(1)
    col = lax.axis_index("pcol").astype(jnp.int32).reshape(1)
    piv = pivots.reshape(1, count)
    params = pltpu.CompilerParams(vmem_limit_bytes=VMEM_BYTES)
    smem = pl.BlockSpec(memory_space=pltpu.SMEM)
    vmem = pl.BlockSpec(memory_space=pltpu.VMEM)
    hbm = pl.BlockSpec(memory_space=pltpu.HBM)

    relayed = list(range(4, devices, 2))
    crossed = [step for step in relayed if step % 4 == 2]
    packing = _Packing(capacity, cols_dev)
    packed_type = jax.ShapeDtypeStruct(packing.shape, F32)
    pick = pl.pallas_call(
        functools.partial(_pick_kernel, devices, block, rows_dev),
        out_shape=jax.ShapeDtypeStruct(((devices - 1) * block, rows_dev), BF16),
        in_specs=[smem, vmem],
        out_specs=vmem,
        compiler_params=params,
        cost_estimate=_cost(PICK_US),
        name="pick_rows",
    )(me, piv)
    outgoing = pl.pallas_call(
        functools.partial(_outgoing_kernel, devices, block, packing),
        out_shape=[jax.ShapeDtypeStruct((block, cols_dev), F32)] + [packed_type] * (devices - 1),
        in_specs=[smem, vmem, vmem],
        out_specs=[vmem] * devices,
        compiler_params=params,
        name="outgoing_rows",
    )(me, pick, slab)

    def swap(x, axis, size, step):
        return lax.ppermute(x, axis, [(i, i ^ step) for i in range(size)])

    direct = [1, 2] + relayed + [3]
    rows = {0: outgoing[0]}
    for step in direct:
        if step in crossed:
            ends = {0: step ^ 1, 1: step, step: 1, step ^ 1: 0}
            pairs = [(i, ends.get(i, i ^ step)) for i in range(devices)]
            rows[step] = lax.ppermute(outgoing[step ^ 1], "prow", pairs)
        else:
            rows[step] = swap(outgoing[step], "prow", devices, step)
    order = [0] + direct + [step ^ 1 for step in relayed]
    early = 1 + len(direct)
    late = devices - early
    panel = pl.pallas_call(
        _after_kernel,
        out_shape=jax.ShapeDtypeStruct(panel.shape, F32),
        in_specs=[vmem, pl.BlockSpec(memory_space=pl.ANY)],
        out_specs=vmem,
        compiler_params=params,
        cost_estimate=_cost(AFTER_US),
        name="panel_after",
    )(panel, rows[2])
    panels = {0: panel}
    for step in range(2, pieces, 2):
        panels[step] = swap(panels[0], "pcol", pieces, step)
    for step in range(0, pieces, 2):
        panels[step ^ 1] = swap(panels[step], "pcol", pieces, 1)

    high_early, low_early, high_late, low_late, kept = pl.pallas_call(
        functools.partial(_factor_kernel, devices, block, order, early, crossed, pieces),
        out_shape=[jax.ShapeDtypeStruct((rows_dev, k * block), BF16) for k in (early, early, late, late)]
        + [jax.ShapeDtypeStruct((rows_dev, cols_dev), F32)],
        in_specs=[smem, smem, vmem, vmem, vmem] + [vmem] * pieces,
        out_specs=[vmem] * 5,
        scratch_shapes=[
            pltpu.VMEM((rows_dev, count), F32),
            pltpu.VMEM((count, count), F32),
            pltpu.VMEM((rows_dev, count), F32),
        ],
        compiler_params=params,
        cost_estimate=_cost(FACTOR_US),
        name="left_factor",
    )(me, col, piv, slab, tri_inverse, *[panels[s] for s in range(pieces)])

    for step in relayed:
        other = step ^ 1
        if step in crossed:
            ends = {0: step, other: 1}
            blocks = {0: outgoing[step], other: outgoing[step]}
        else:
            ends = {0: other, step: 1}
            blocks = {0: outgoing[other], step: outgoing[other]}
        waits = [rows[1], rows[3]] if step == relayed[0] else []
        passed = pl.pallas_call(
            functools.partial(_relay_kernel, list(blocks), len(waits)),
            out_shape=packed_type,
            in_specs=[smem, vmem] + [pl.BlockSpec(memory_space=pl.ANY)] * len(waits) + [vmem] * len(blocks),
            out_specs=vmem,
            compiler_params=params,
            cost_estimate=_cost(RELAY_US),
            name="relay",
        )(me, rows[step], *waits, *blocks.values())
        pairs = [(i, ends.get(i, i ^ 1)) for i in range(devices)]
        rows[other] = lax.ppermute(passed, "prow", pairs)

    result_type = jax.ShapeDtypeStruct((rows_dev, cols_dev), F32)
    high_rows, low_rows = pl.pallas_call(
        functools.partial(_assemble_kernel, block, packing, early),
        out_shape=[jax.ShapeDtypeStruct((early * block, cols_dev), BF16)] * 2,
        in_specs=[vmem] * early,
        out_specs=[vmem] * 2,
        compiler_params=params,
        cost_estimate=_cost(ASSEMBLE_US),
        name="assemble_rows",
    )(*[rows[s] for s in order[:early]])
    partial = pl.pallas_call(
        _early_kernel,
        out_shape=result_type,
        in_specs=[vmem] * 5,
        out_specs=vmem,
        compiler_params=params,
        name="early_rows",
    )(high_early, low_early, kept, high_rows, low_rows)
    rest_high, rest_low = pl.pallas_call(
        functools.partial(_assemble_kernel, block, packing, late - 1),
        out_shape=[jax.ShapeDtypeStruct(((late - 1) * block, cols_dev), BF16)] * 2,
        in_specs=[vmem] * (late - 1),
        out_specs=[vmem] * 2,
        compiler_params=params,
        cost_estimate=_cost(AFTER_US),
        name="assemble_late",
    )(*[rows[s] for s in order[early + 1 :]])
    return pl.pallas_call(
        functools.partial(_late_kernel, block, packing, late),
        out_shape=result_type,
        in_specs=[vmem] * 6,
        out_specs=hbm,
        scratch_shapes=[pltpu.VMEM((late * block, cols_dev), BF16)] * 2
        + [pltpu.VMEM((rows_dev, cols_dev), F32), pltpu.SemaphoreType.DMA((STORE_PARTS,))],
        compiler_params=params,
        name="late_rows",
    )(high_late, low_late, partial, rows[order[early]], rest_high, rest_low)


def solution(mesh):
    return jax.shard_map(
        per_device,
        mesh=mesh,
        in_specs=(P("prow", "pcol"), P("prow", "pcol"), P(), P()),
        out_specs=P("prow", "pcol"),
        check_vma=False,
    )
```
